32 devices in a mesh: ctx: 16 (over z, y, x), fsdp: 2 (over core).
Axes of the slice: x: 2, y: 2, z: 4, core: 2. Of those that a mesh axis runs over, the one named last changes fastest.
Arguments:
- tokens: bfloat16 [4, 2048, 1024], P('fsdp', 'ctx'), may hold values from -6 to 6
- grad_out: bfloat16 [4, 2048, 1024], P('fsdp', 'ctx'), may hold values from -6 to 6
- ln1_gain: bfloat16 [1024], P('fsdp'), may hold values from 0.5 to 1.5
- ln1_bias: bfloat16 [1024], P('fsdp'), may hold values from -3 to 3
- w_qkv: bfloat16 [1024, 3072], P('fsdp'), may hold values from -0.1875 to 0.1875
- b_query: bfloat16 [1024], P('fsdp'), may hold values from -3 to 3
- b_value: bfloat16 [1024], P('fsdp'), may hold values from -0.29882812 to 0.29882812
- w_out: bfloat16 [1024, 1024], P('fsdp'), may hold values from -2 to 2
- b_out: bfloat16 [1024], P('fsdp'), may hold values from -3 to 3
- ln2_gain: bfloat16 [1024], P('fsdp'), may hold values from 0.5 to 1.5
- ln2_bias: bfloat16 [1024], P('fsdp'), may hold values from -3 to 3
- w_fc: bfloat16 [1024, 4096], P('fsdp'), may hold values from -0.1875 to 0.1875
- b_fc: bfloat16 [4096], P('fsdp'), may hold values from -3 to 3
- w_proj: bfloat16 [4096, 1024], P('fsdp'), may hold values from -0.09375 to 0.09375
- b_proj: bfloat16 [1024], P('fsdp'), may hold values from -3 to 3
Outputs:
- output: bfloat16 [4, 2048, 1024], P('fsdp', 'ctx')
- grad_tokens: bfloat16 [4, 2048, 1024], P('fsdp', 'ctx')
- grad_ln1_gain: float32 [1024], P('fsdp')
- grad_ln1_bias: float32 [1024], P('fsdp')
- grad_w_qkv: float32 [1024, 3072], P('fsdp')
- grad_b_query: float32 [1024], P('fsdp')
- grad_b_value: float32 [1024], P('fsdp')
- grad_w_out: float32 [1024, 1024], P('fsdp')
- grad_b_out: float32 [1024], P('fsdp')
- grad_ln2_gain: float32 [1024], P('fsdp')
- grad_ln2_bias: float32 [1024], P('fsdp')
- grad_w_fc: float32 [1024, 4096], P('fsdp')
- grad_b_fc: float32 [4096], P('fsdp')
- grad_w_proj: float32 [4096, 1024], P('fsdp')
- grad_b_proj: float32 [1024], P('fsdp')
The draws below stay inside these ranges and needn't reach their ends.
All inputs are finite; a program needn't handle non-finite values.
Results may differ from the reference program's by a relative error of at most 0.017.
Values may be sent and summed in bfloat16 or wider, within the bound.
A program may use at most 384 MiB of HBM per device.

```python
import math
import jax
import jax.numpy as jnp
from jax import lax

D = 1024
HEADS = 16
HEAD = 64
FF = 4096
SEQS = 4
LEN = 2048


def block_levels(rng, dims, split, low, top_value):
    level, own = 1.0, jax.random.fold_in(rng, 6)
    for axis_at, shards_of in split:
        heights = jnp.exp(jax.random.uniform(jax.random.fold_in(own, axis_at), (shards_of,), jnp.float32, low / len(split), top_value / len(split)))
        level = level * jnp.repeat(heights, dims[axis_at] // shards_of).reshape([-1 if axis == axis_at else 1 for axis in range(len(dims))])
    return level


def noise(key, extent, scale, reach, pieces=(), kind=jnp.bfloat16):
    values = jax.random.normal(key, extent, jnp.float32) * scale
    if len(pieces) > 0:
        values = block_levels(key, extent, pieces, -0.22, 0.18) * values
    return jnp.clip(values, min=-reach, max=reach).astype(kind)


def setup_inputs(seed: int = 0) -> dict:
    key_list = jax.random.split(jax.random.key(seed), 16)
    return {
        "tokens": noise(key_list[0], (SEQS, LEN, D), 1.0, 6.0, ((0, 2), (1, 16))),
        "grad_out": noise(key_list[1], (SEQS, LEN, D), 1.0, 6.0, ((0, 2), (1, 16))),
        "ln1_gain": jnp.clip(1.0 + 0.1 * jax.random.normal(key_list[2], (D,), jnp.float32), 0.5, 1.5).astype(jnp.bfloat16),
        "ln1_bias": noise(key_list[3], (D,), 0.3, 3.0, ((0, 2),)),
        "w_qkv": noise(key_list[4], (D, 3 * D), D ** -0.5, 0.1875, ((0, 2),)),
        "b_query": noise(key_list[5], (D,), 0.3, 3.0, ((0, 2),)),
        "b_value": noise(key_list[6], (D,), 0.05, 0.29882812, ((0, 2),)),
        "w_out": noise(key_list[7], (D, D), (max(4, D // 128)) ** -0.5, 2.0, ((0, 2),)),
        "b_out": noise(key_list[8], (D,), 0.3, 3.0, ((0, 2),)),
        "ln2_gain": jnp.clip(1.0 + 0.1 * jax.random.normal(key_list[9], (D,), jnp.float32), 0.5, 1.5).astype(jnp.bfloat16),
        "ln2_bias": noise(key_list[10], (D,), 0.3, 3.0, ((0, 2),)),
        "w_fc": noise(key_list[11], (D, FF), D ** -0.5, 0.1875, ((0, 2),)),
        "b_fc": noise(key_list[12], (FF,), 0.5, 3.0, ((0, 2),)),
        "w_proj": noise(key_list[13], (FF, D), FF ** -0.5, 0.09375, ((0, 2),)),
        "b_proj": noise(key_list[14], (D,), 0.3, 3.0, ((0, 2),)),
    }


@jax.custom_vjp
def low(v):
    return lax.optimization_barrier(v.astype(jnp.bfloat16)).astype(jnp.float32)

@jax.custom_vjp
def low_back(v):
    return v

def low_keep(v):
    return (low(v), None)

def low_pass(kept, grad):
    return (grad,)

def back_keep(v):
    return (v, None)

def back_low(kept, grad):
    return (low(grad),)
low.defvjp(low_keep, low_pass)
low_back.defvjp(back_keep, back_low)

def matmul(left, right):
    return jnp.dot(left, right, precision=lax.Precision.HIGHEST, preferred_element_type=jnp.float32)

def rounded_both(value):
    return low_back(low(value))

def norm(inputs, gain, shift):
    mean = lax.optimization_barrier(jnp.mean(inputs, axis=-1, keepdims=True))
    centred = inputs - mean
    spread = lax.optimization_barrier(jnp.mean(centred * centred, axis=-1, keepdims=True))
    return centred * lax.rsqrt(spread + 1e-05) * gain + shift

def attend(query, keys, values):
    length = query.shape[1]
    size = min(512, length)
    count = length // size
    scale = 1.0 / math.sqrt(HEAD)
    blocks = query.reshape(HEADS, count, size, HEAD).transpose(1, 0, 2, 3)
    key_pos = jnp.arange(length, dtype=jnp.int32)

    def one_block(item):
        query_block, index = item
        scores = low_back(jnp.einsum('hqd,hkd->hqk', query_block, keys, precision=lax.Precision.HIGHEST) * scale)
        query_pos = index * size + jnp.arange(size, dtype=jnp.int32)
        allowed = key_pos[None, :] <= query_pos[:, None]
        masked = jnp.where(allowed[None], scores, -1e+30)
        top = lax.optimization_barrier(jnp.max(masked, axis=-1, keepdims=True))
        weights = jnp.where(allowed[None], jnp.exp(masked - top), 0.0)
        probs = weights / lax.optimization_barrier(jnp.sum(weights, axis=-1, keepdims=True))
        return jnp.einsum('hqk,hkd->hqd', low(probs), values, precision=lax.Precision.HIGHEST)
    result = lax.map(jax.checkpoint(one_block), (blocks, jnp.arange(count, dtype=jnp.int32)))
    return result.transpose(1, 0, 2, 3).reshape(HEADS, length, HEAD)

def layer(inputs, params):
    gain_one, shift_one, wide_qkv, bias_query, bias_value, wide_out, bias_out, gain_two, shift_two, wide_fc, bias_fc, wide_proj, bias_proj = params
    normed_one = low(norm(inputs, gain_one, shift_one))
    packed = matmul(normed_one, wide_qkv)
    query = rounded_both(packed[:, :D] + bias_query)
    keys = rounded_both(packed[:, D:2 * D])
    values = rounded_both(packed[:, 2 * D:] + bias_value)

    def heads_of(item):
        return item.reshape(-1, HEADS, HEAD).transpose(1, 0, 2)
    attended = attend(heads_of(query), heads_of(keys), heads_of(values))
    attended = rounded_both(attended.transpose(1, 0, 2).reshape(-1, D))
    mixed = inputs + low_back(matmul(attended, wide_out) + bias_out)
    normed_two = low(norm(mixed, gain_two, shift_two))
    hidden = low_back(matmul(normed_two, wide_fc) + bias_fc)
    activated = low(jax.nn.gelu(hidden, approximate=True))
    return mixed + matmul(activated, wide_proj) + bias_proj

def reference(tokens, grad_out, ln1_gain, ln1_bias, w_qkv, b_query, b_value, w_out, b_out, ln2_gain, ln2_bias, w_fc, b_fc, w_proj, b_proj):
    params = tuple((item.astype(jnp.float32) for item in (ln1_gain, ln1_bias, w_qkv, b_query, b_value, w_out, b_out, ln2_gain, ln2_bias, w_fc, b_fc, w_proj, b_proj)))

    def step(totals, item):
        sequence, cotangent = item
        result, backward = jax.vjp(layer, sequence.astype(jnp.float32), params)
        grad_input, grad_params = backward(cotangent.astype(jnp.float32))
        totals = jax.tree.map(jnp.add, totals, grad_params)
        return (totals, (result.astype(jnp.bfloat16), grad_input.astype(jnp.bfloat16)))
    zeros = jax.tree.map(jnp.zeros_like, params)
    totals, (results, grad_inputs) = lax.scan(step, zeros, (tokens, grad_out))
    return (results, grad_inputs, totals[0], totals[1], totals[2], totals[3], totals[4], totals[5], totals[6], totals[7], totals[8], totals[9], totals[10], totals[11], totals[12])
```

```python
from functools import partial
import math

import jax
import jax.numpy as jnp
from jax import lax
from jax.experimental import pallas as pl
from jax.experimental.pallas import tpu as pltpu
from jax.sharding import PartitionSpec as P

HEADS = 16


def norm(inputs, gain, shift):
    mean = jnp.mean(inputs, axis=-1, keepdims=True)
    centred = inputs - mean
    spread = jnp.mean(centred * centred, axis=-1, keepdims=True)
    return centred * lax.rsqrt(spread + 1e-05) * gain + shift


def inner(left, right):
    return lax.dot_general(
        left, right, (((0,), (0,)), ((), ())), preferred_element_type=jnp.float32
    )


def times_transposed(left, right):
    return lax.dot_general(
        left, right, (((1,), (1,)), ((), ())), preferred_element_type=jnp.float32
    )


def dot_nt(left, right):
    return lax.dot_general(
        left, right, (((1,), (1,)), ((), ())), preferred_element_type=jnp.float32
    )


def dot_nn(left, right):
    return jnp.dot(left, right, preferred_element_type=jnp.float32)


def causal(scores_t, start):
    rows, size = scores_t.shape
    key = lax.broadcasted_iota(jnp.int32, (size, size), 0)
    pos = lax.broadcasted_iota(jnp.int32, (size, size), 1)
    last = jnp.where(key <= pos, scores_t[start:], -1e30)
    if start == 0:
        return last
    return jnp.concatenate([scores_t[:start], last], axis=0)


def forward_kernel(head_size, size, packed_ref, out_ref, keep_ref, lse_ref):
    chips, _, block, span = packed_ref.shape
    length = chips * block
    query = packed_ref[:, 0].reshape(length, span)
    keys = packed_ref[:, 1].reshape(length, span)
    values = packed_ref[:, 2].reshape(length, span)
    for first in range(0, length, size):
        stop = first + size
        parts = []
        for head in range(span // head_size):
            cols = slice(head * head_size, (head + 1) * head_size)
            scores = causal(dot_nt(keys[:stop, cols], query[first:stop, cols]), first)
            top = jnp.max(scores, axis=0, keepdims=True)
            weights = jnp.exp(scores - top)
            total = jnp.sum(weights, axis=0, keepdims=True)
            summed = lax.dot_general(
                values[:stop, cols],
                weights.astype(jnp.bfloat16),
                (((0,), (0,)), ((), ())),
                preferred_element_type=jnp.float32,
            )
            attended = summed / total
            keep_ref[head, :, first:stop] = attended
            lse_ref[head, :, first:stop] = top + jnp.log(total)
            parts.append(attended)
        joined = parts[0] if len(parts) == 1 else jnp.concatenate(parts, axis=0)
        out_ref[first // block : stop // block] = (
            joined.T.astype(jnp.bfloat16).reshape(size // block, block, span)
        )


def backward_kernel(head_size, size, packed_ref, grad_ref, keep_ref, lse_ref, out_ref, key_acc, value_acc):
    chips, _, block, span = packed_ref.shape
    length = chips * block
    query = packed_ref[:, 0].reshape(length, span)
    keys = packed_ref[:, 1].reshape(length, span)
    values = packed_ref[:, 2].reshape(length, span)
    grads = grad_ref[...].reshape(length, span)
    key_acc[...] = jnp.zeros_like(key_acc)
    value_acc[...] = jnp.zeros_like(value_acc)
    for first in range(0, length, size):
        stop = first + size
        grad_t = grads[first:stop].astype(jnp.float32).T
        parts = []
        for head in range(span // head_size):
            cols = slice(head * head_size, (head + 1) * head_size)
            q, do = query[first:stop, cols], grads[first:stop, cols]
            k, v = keys[:stop, cols], values[:stop, cols]
            delta = jnp.sum(grad_t[cols] * keep_ref[head, :, first:stop], axis=0, keepdims=True)
            scores = causal(dot_nt(k, q), first)
            probs = jnp.exp(scores - lse_ref[head, :, first:stop])
            value_acc[head, :stop] += dot_nn(probs.astype(jnp.bfloat16), do)
            slopes = (probs * (dot_nt(v, do) - delta)).astype(jnp.bfloat16)
            key_acc[head, :stop] += dot_nn(slopes, q)
            parts.append(
                lax.dot_general(
                    k, slopes, (((0,), (0,)), ((), ())), preferred_element_type=jnp.float32
                )
            )
        joined = parts[0] if len(parts) == 1 else jnp.concatenate(parts, axis=0)
        grad_query = (joined * (1.0 / math.sqrt(head_size))).T
        out_ref[first // block : stop // block, 0] = (
            grad_query.astype(jnp.bfloat16).reshape(size // block, block, span)
        )
    for at, acc in ((1, key_acc), (2, value_acc)):
        heads = [acc[head] for head in range(span // head_size)]
        whole = heads[0] if len(heads) == 1 else jnp.concatenate(heads, axis=1)
        out_ref[:, at] = whole.astype(jnp.bfloat16).reshape(chips, block, span)


def attend_forward(packed, head_size):
    chips, _, block, span = packed.shape
    length, heads = chips * block, span // head_size
    pairs = heads * length * length
    return pl.pallas_call(
        partial(forward_kernel, head_size, min(512, length)),
        out_shape=(
            jax.ShapeDtypeStruct((chips, block, span), jnp.bfloat16),
            jax.ShapeDtypeStruct((heads, head_size, length), jnp.float32),
            jax.ShapeDtypeStruct((heads, 1, length), jnp.float32),
        ),
        compiler_params=pltpu.CompilerParams(vmem_limit_bytes=56 * 2**20),
        cost_estimate=pl.CostEstimate(
            flops=3 * pairs * head_size, bytes_accessed=6 * packed.size, transcendentals=pairs
        ),
        name="attend_forward",
    )(packed)


def attend_backward(packed, grads, kept, lse, head_size):
    chips, _, block, span = packed.shape
    length, heads = chips * block, span // head_size
    pairs = heads * length * length
    return pl.pallas_call(
        partial(backward_kernel, head_size, min(512, length)),
        out_shape=jax.ShapeDtypeStruct(packed.shape, jnp.bfloat16),
        scratch_shapes=[
            pltpu.VMEM((heads, length, head_size), jnp.float32),
            pltpu.VMEM((heads, length, head_size), jnp.float32),
        ],
        compiler_params=pltpu.CompilerParams(vmem_limit_bytes=56 * 2**20),
        cost_estimate=pl.CostEstimate(
            flops=8 * pairs * head_size, bytes_accessed=8 * packed.size, transcendentals=pairs
        ),
        name="attend_backward",
    )(packed, grads, kept, lse)


def to_heads(arrays, chips):
    seqs, block, width = arrays[0].shape
    span = seqs * width // chips
    parts = [
        item.reshape(seqs, block, width // span, span)
        .transpose(0, 2, 1, 3)
        .reshape(chips, block, span)
        for item in arrays
    ]
    return lax.all_to_all(jnp.stack(parts, axis=1), "ctx", 0, 0, tiled=True)


def to_tokens(item, seqs, width):
    chips, count, block, span = item.shape
    back = lax.all_to_all(item, "ctx", 0, 0, tiled=True)
    back = back.reshape(seqs, width // span, count, block, span).transpose(2, 0, 3, 1, 4)
    return back.reshape(count, seqs * block, width)


def reduce_rows(grad):
    part = lax.psum_scatter(grad.astype(jnp.bfloat16), "fsdp", scatter_dimension=0, tiled=True)
    part = lax.psum_scatter(part, "ctx", scatter_dimension=0, tiled=True)
    return lax.all_gather(part, "ctx", axis=0, tiled=True)


def local(
    tokens,
    grad_out,
    ln1_gain,
    ln1_bias,
    w_qkv,
    b_query,
    b_value,
    w_out,
    b_out,
    ln2_gain,
    ln2_bias,
    w_fc,
    b_fc,
    w_proj,
    b_proj,
):
    fsdp = lax.axis_size("fsdp")
    chips = lax.axis_size("ctx")
    vectors = (ln1_gain, ln1_bias, b_query, b_value, b_out, ln2_gain, ln2_bias, b_proj, b_fc)
    edges = [0]
    for item in vectors:
        edges.append(edges[-1] + item.shape[0])
    wide_qkv = lax.all_gather(w_qkv, "fsdp", axis=0, tiled=True)
    joined = lax.all_gather(jnp.concatenate(vectors).reshape(-1, 128), "fsdp", axis=0, tiled=True)
    joined = joined.reshape(fsdp, edges[-1])
    (gain_one, shift_one, bias_query, bias_value, bias_out, gain_two, shift_two, bias_proj, bias_fc) = (
        joined[:, at:to].reshape(-1) for at, to in zip(edges[:-1], edges[1:])
    )
    wide_out = lax.all_gather(w_out, "fsdp", axis=0, tiled=True)
    wide_fc = lax.all_gather(w_fc, "fsdp", axis=0, tiled=True)
    wide_proj = lax.all_gather(w_proj, "fsdp", axis=0, tiled=True)
    gain_one = gain_one.astype(jnp.float32)
    shift_one = shift_one.astype(jnp.float32)
    gain_two = gain_two.astype(jnp.float32)
    shift_two = shift_two.astype(jnp.float32)
    seqs, block, width = tokens.shape
    rows = seqs * block
    heads = HEADS
    head_size = width // heads
    scale = 1.0 / math.sqrt(head_size)
    inputs = tokens.astype(jnp.float32).reshape(rows, width)
    low_one = norm(inputs, gain_one, shift_one).astype(jnp.bfloat16)
    packed = jnp.dot(low_one, wide_qkv, preferred_element_type=jnp.float32)
    query = (packed[:, :width] + bias_query.astype(jnp.float32)).astype(jnp.bfloat16)
    keys = packed[:, width : 2 * width].astype(jnp.bfloat16)
    values = (packed[:, 2 * width :] + bias_value.astype(jnp.float32)).astype(jnp.bfloat16)
    query = query * jnp.asarray(scale, jnp.bfloat16)
    shape = (seqs, block, width)
    packed_heads = to_heads(
        (query.reshape(shape), keys.reshape(shape), values.reshape(shape)), chips
    )
    attended, kept, row_lse = attend_forward(packed_heads, head_size)
    low_att = to_tokens(attended[:, None], seqs, width)[0]
    mixed = (
        inputs
        + jnp.dot(low_att, wide_out, preferred_element_type=jnp.float32)
        + bias_out.astype(jnp.float32)
    )
    low_two = norm(mixed, gain_two, shift_two).astype(jnp.bfloat16)
    hidden = jnp.dot(low_two, wide_fc, preferred_element_type=jnp.float32) + bias_fc.astype(
        jnp.float32
    )
    low_act = jax.nn.gelu(hidden, approximate=True).astype(jnp.bfloat16)
    result = (
        mixed
        + jnp.dot(low_act, wide_proj, preferred_element_type=jnp.float32)
        + bias_proj.astype(jnp.float32)
    )
    output = result.astype(jnp.bfloat16).reshape(seqs, block, width)
    grad_rows = grad_out.reshape(rows, width)
    grad_float = grad_rows.astype(jnp.float32)
    grad_b_proj = jnp.sum(grad_float, axis=0)
    grad_w_proj = inner(low_act, grad_rows)
    grad_act = times_transposed(grad_rows, wide_proj)
    _, gelu_back = jax.vjp(partial(jax.nn.gelu, approximate=True), hidden)
    low_hidden = gelu_back(grad_act)[0].astype(jnp.bfloat16)
    grad_b_fc = jnp.sum(low_hidden.astype(jnp.float32), axis=0)
    grad_w_fc = inner(low_two, low_hidden)
    grad_normed_two = times_transposed(low_hidden, wide_fc)
    _, norm_two_back = jax.vjp(norm, mixed, gain_two, shift_two)
    grad_mixed_part, grad_ln2_gain, grad_ln2_bias = norm_two_back(grad_normed_two)
    grad_mixed = grad_float + grad_mixed_part
    low_branch = grad_mixed.astype(jnp.bfloat16)
    grad_b_out = jnp.sum(low_branch.astype(jnp.float32), axis=0)
    grad_w_out = inner(low_att, low_branch)
    low_grad_att = times_transposed(low_branch, wide_out).astype(jnp.bfloat16).reshape(shape)
    grad_heads = to_heads((low_grad_att,), chips)[:, 0]
    grads = attend_backward(packed_heads, grad_heads, kept, row_lse, head_size)
    low_grad_query, low_grad_keys, low_grad_values = to_tokens(grads, seqs, width)
    grad_b_query = jnp.sum(low_grad_query.astype(jnp.float32), axis=0)
    grad_b_value = jnp.sum(low_grad_values.astype(jnp.float32), axis=0)
    grad_packed = jnp.concatenate([low_grad_query, low_grad_keys, low_grad_values], axis=1)
    grad_w_qkv = inner(low_one, grad_packed)
    grad_normed_one = times_transposed(grad_packed, wide_qkv)
    _, norm_one_back = jax.vjp(norm, inputs, gain_one, shift_one)
    grad_input_part, grad_ln1_gain, grad_ln1_bias = norm_one_back(grad_normed_one)
    grad_tokens = (grad_mixed + grad_input_part).astype(jnp.bfloat16).reshape(seqs, block, width)
    small = (
        grad_ln1_gain,
        grad_ln1_bias,
        grad_b_query,
        grad_b_value,
        grad_b_out,
        grad_ln2_gain,
        grad_ln2_bias,
        grad_b_proj,
        grad_b_fc,
    )
    small = jnp.concatenate([item.reshape(fsdp, -1) for item in small], axis=1)
    small = small.reshape(fsdp, -1, 128)
    spare = -small.shape[1] % (16 * chips)
    small = jnp.pad(small, ((0, 0), (0, spare), (0, 0)))
    out_rows = w_out.size // 128
    tail = jnp.concatenate([grad_w_out.reshape(fsdp, out_rows, 128), small], axis=1)
    tail = reduce_rows(tail.reshape(-1, 128)).astype(jnp.float32)
    total_out = tail[:out_rows].reshape(w_out.shape)
    rest = tail[out_rows:].reshape(-1)
    part = [rest[at:to] for at, to in zip(edges[:-1], edges[1:])]
    total_qkv = reduce_rows(grad_w_qkv).astype(jnp.float32)
    total_fc = reduce_rows(grad_w_fc).astype(jnp.float32)
    total_proj = reduce_rows(grad_w_proj).astype(jnp.float32)
    return (
        output,
        grad_tokens,
        part[0],
        part[1],
        total_qkv,
        part[2],
        part[3],
        total_out,
        part[4],
        part[5],
        part[6],
        total_fc,
        part[8],
        total_proj,
        part[7],
    )


def solution(mesh):
    in_specs = (
        P("fsdp", "ctx", None),
        P("fsdp", "ctx", None),
        P("fsdp"),
        P("fsdp"),
        P("fsdp", None),
        P("fsdp"),
        P("fsdp"),
        P("fsdp", None),
        P("fsdp"),
        P("fsdp"),
        P("fsdp"),
        P("fsdp", None),
        P("fsdp"),
        P("fsdp", None),
        P("fsdp"),
    )
    out_specs = (
        P("fsdp", "ctx", None),
        P("fsdp", "ctx", None),
        P("fsdp"),
        P("fsdp"),
        P("fsdp", None),
        P("fsdp"),
        P("fsdp"),
        P("fsdp", None),
        P("fsdp"),
        P("fsdp"),
        P("fsdp"),
        P("fsdp", None),
        P("fsdp"),
        P("fsdp", None),
        P("fsdp"),
    )
    return jax.shard_map(local, mesh=mesh, in_specs=in_specs, out_specs=out_specs, check_vma=False)
```

```python
from functools import partial
import math

import jax
import jax.numpy as jnp
from jax import lax
from jax.experimental import pallas as pl
from jax.experimental.pallas import tpu as pltpu
from jax.sharding import PartitionSpec as P

HEADS = 16


def norm(inputs, gain, shift):
    mean = jnp.mean(inputs, axis=-1, keepdims=True)
    centred = inputs - mean
    spread = jnp.mean(centred * centred, axis=-1, keepdims=True)
    return centred * lax.rsqrt(spread + 1e-05) * gain + shift


def inner(left, right):
    return lax.dot_general(
        left, right, (((0,), (0,)), ((), ())), preferred_element_type=jnp.float32
    )


def times_transposed(left, right):
    return lax.dot_general(
        left, right, (((1,), (1,)), ((), ())), preferred_element_type=jnp.float32
    )


def dot_nt(left, right):
    return lax.dot_general(
        left, right, (((1,), (1,)), ((), ())), preferred_element_type=jnp.float32
    )


def dot_nn(left, right):
    return jnp.dot(left, right, preferred_element_type=jnp.float32)


def causal(scores_t, start):
    rows, size = scores_t.shape
    key = lax.broadcasted_iota(jnp.int32, (size, size), 0)
    pos = lax.broadcasted_iota(jnp.int32, (size, size), 1)
    last = jnp.where(key <= pos, scores_t[start:], -1e30)
    if start == 0:
        return last
    return jnp.concatenate([scores_t[:start], last], axis=0)


def forward_kernel(head_size, size, packed_ref, out_ref, keep_ref, lse_ref):
    chips, _, block, span = packed_ref.shape
    length = chips * block
    query = packed_ref[:, 0].reshape(length, span)
    keys = packed_ref[:, 1].reshape(length, span)
    values = packed_ref[:, 2].reshape(length, span)
    for first in range(0, length, size):
        stop = first + size
        parts = []
        for head in range(span // head_size):
            cols = slice(head * head_size, (head + 1) * head_size)
            scores = causal(dot_nt(keys[:stop, cols], query[first:stop, cols]), first)
            top = jnp.max(scores, axis=0, keepdims=True)
            weights = jnp.exp(scores - top)
            total = jnp.sum(weights, axis=0, keepdims=True)
            summed = lax.dot_general(
                values[:stop, cols],
                weights.astype(jnp.bfloat16),
                (((0,), (0,)), ((), ())),
                preferred_element_type=jnp.float32,
            )
            attended = summed / total
            keep_ref[head, :, first:stop] = attended
            lse_ref[head, :, first:stop] = top + jnp.log(total)
            parts.append(attended)
        joined = parts[0] if len(parts) == 1 else jnp.concatenate(parts, axis=0)
        out_ref[first // block : stop // block] = (
            joined.T.astype(jnp.bfloat16).reshape(size // block, block, span)
        )


def backward_kernel(head_size, size, packed_ref, grad_ref, keep_ref, lse_ref, out_ref, key_acc, value_acc):
    chips, _, block, span = packed_ref.shape
    length = chips * block
    query = packed_ref[:, 0].reshape(length, span)
    keys = packed_ref[:, 1].reshape(length, span)
    values = packed_ref[:, 2].reshape(length, span)
    grads = grad_ref[...].reshape(length, span)
    key_acc[...] = jnp.zeros_like(key_acc)
    value_acc[...] = jnp.zeros_like(value_acc)
    for first in range(0, length, size):
        stop = first + size
        grad_t = grads[first:stop].astype(jnp.float32).T
        parts = []
        for head in range(span // head_size):
            cols = slice(head * head_size, (head + 1) * head_size)
            q, do = query[first:stop, cols], grads[first:stop, cols]
            k, v = keys[:stop, cols], values[:stop, cols]
            delta = jnp.sum(grad_t[cols] * keep_ref[head, :, first:stop], axis=0, keepdims=True)
            scores = causal(dot_nt(k, q), first)
            probs = jnp.exp(scores - lse_ref[head, :, first:stop])
            value_acc[head, :stop] += dot_nn(probs.astype(jnp.bfloat16), do)
            slopes = (probs * (dot_nt(v, do) - delta)).astype(jnp.bfloat16)
            key_acc[head, :stop] += dot_nn(slopes, q)
            parts.append(
                lax.dot_general(
                    k, slopes, (((0,), (0,)), ((), ())), preferred_element_type=jnp.float32
                )
            )
        joined = parts[0] if len(parts) == 1 else jnp.concatenate(parts, axis=0)
        grad_query = (joined * (1.0 / math.sqrt(head_size))).T
        out_ref[first // block : stop // block, 0] = (
            grad_query.astype(jnp.bfloat16).reshape(size // block, block, span)
        )
    for at, acc in ((1, key_acc), (2, value_acc)):
        heads = [acc[head] for head in range(span // head_size)]
        whole = heads[0] if len(heads) == 1 else jnp.concatenate(heads, axis=1)
        out_ref[:, at] = whole.astype(jnp.bfloat16).reshape(chips, block, span)


def attend_forward(packed, head_size):
    chips, _, block, span = packed.shape
    length, heads = chips * block, span // head_size
    pairs = heads * length * length
    return pl.pallas_call(
        partial(forward_kernel, head_size, min(512, length)),
        out_shape=(
            jax.ShapeDtypeStruct((chips, block, span), jnp.bfloat16),
            jax.ShapeDtypeStruct((heads, head_size, length), jnp.float32),
            jax.ShapeDtypeStruct((heads, 1, length), jnp.float32),
        ),
        compiler_params=pltpu.CompilerParams(vmem_limit_bytes=56 * 2**20),
        cost_estimate=pl.CostEstimate(
            flops=3 * pairs * head_size, bytes_accessed=6 * packed.size, transcendentals=pairs
        ),
        name="attend_forward",
    )(packed)


def attend_backward(packed, grads, kept, lse, head_size):
    chips, _, block, span = packed.shape
    length, heads = chips * block, span // head_size
    pairs = heads * length * length
    return pl.pallas_call(
        partial(backward_kernel, head_size, min(512, length)),
        out_shape=jax.ShapeDtypeStruct(packed.shape, jnp.bfloat16),
        scratch_shapes=[
            pltpu.VMEM((heads, length, head_size), jnp.float32),
            pltpu.VMEM((heads, length, head_size), jnp.float32),
        ],
        compiler_params=pltpu.CompilerParams(vmem_limit_bytes=56 * 2**20),
        cost_estimate=pl.CostEstimate(
            flops=8 * pairs * head_size, bytes_accessed=8 * packed.size, transcendentals=pairs
        ),
        name="attend_backward",
    )(packed, grads, kept, lse)


def to_heads(arrays, chips):
    seqs, block, width = arrays[0].shape
    span = seqs * width // chips
    parts = [
        item.reshape(seqs, block, width // span, span)
        .transpose(0, 2, 1, 3)
        .reshape(chips, block, span)
        for item in arrays
    ]
    return lax.all_to_all(jnp.stack(parts, axis=1), "ctx", 0, 0, tiled=True)


def to_tokens(item, seqs, width):
    chips, count, block, span = item.shape
    back = lax.all_to_all(item, "ctx", 0, 0, tiled=True)
    back = back.reshape(seqs, width // span, count, block, span).transpose(2, 0, 3, 1, 4)
    return back.reshape(count, seqs * block, width)


def reduce_rows(grad):
    part = lax.psum_scatter(grad.astype(jnp.bfloat16), "fsdp", scatter_dimension=0, tiled=True)
    part = lax.psum_scatter(part, "ctx", scatter_dimension=0, tiled=True)
    return lax.all_gather(part, "ctx", axis=0, tiled=True)


def ring_place(at):
    z, y, x = at // 4, (at // 2) % 2, at % 2
    column = y * (3 - x) + (1 - y) * x
    return column, z


def ring_kernel(
    chips, big, tiny, sum_big, sum_tiny, own, own_tiny, met, met_tiny, hop, hop_tiny,
    own_sem, met_send, met_recv, hop_send, hop_recv, all_send, all_recv,
):
    depth = chips // 4
    core = lax.axis_index("fsdp")
    column, z = ring_place(lax.axis_index("ctx"))
    odd = column % 2
    place = column * depth + (1 - odd) * z + odd * (depth - 1 - z)

    def device(spot):
        column, z = spot // depth, spot % depth
        odd = column % 2
        z = (1 - odd) * z + odd * (depth - 1 - z)
        return {"ctx": z * 4 + (column // 2) * 2 + ((column + 1) // 2) % 2}

    after, before = device((place + 1) % chips), device((place + chips - 1) % chips)
    other = {"fsdp": 1 - core}
    barrier = pltpu.get_barrier_semaphore()
    for peer in (after, before, other):
        pl.semaphore_signal(barrier, inc=1, device_id=peer, device_id_type=pl.DeviceIdType.MESH)
    pl.semaphore_wait(barrier, 3)

    lanes = big.shape[1]
    views = []
    for lane in range(lanes):
        views.append(
            (
                1 - 2 * (lane % 2),
                lambda half, at, lane=lane: big.at[half, lane, at],
                own.at[lane],
                met.at[lane],
                hop.at[lane],
                sum_big.at[lane],
            )
        )
    views.append(
        (1, lambda half, at: tiny.at[half, at], own_tiny, met_tiny, hop_tiny, sum_tiny)
    )

    def chunk(turn, step):
        return (place + turn * step + 2 * chips) % chips

    def remote(source, target, send, recv, peer):
        return pltpu.make_async_remote_copy(
            src_ref=source,
            dst_ref=target,
            send_sem=send,
            recv_sem=recv,
            device_id=peer,
            device_id_type=pl.DeviceIdType.MESH,
        )

    def fetch(lane, step):
        turn, source, mine, theirs, _, _ = views[lane]
        at = chunk(-turn, step)
        return (
            pltpu.make_async_copy(source(core, at), mine.at[at], own_sem.at[lane, step]),
            remote(
                source(1 - core, at),
                theirs.at[at],
                met_send.at[lane, step],
                met_recv.at[lane, step],
                other,
            ),
        )

    def pass_on(lane, step, source):
        turn, slots = views[lane][0], views[lane][4]
        return remote(
            source,
            slots.at[step],
            hop_send.at[lane, step],
            hop_recv.at[lane, step],
            after if turn == 1 else before,
        )

    def share(lane, step):
        turn, total = views[lane][0], views[lane][5]
        at = chunk(-turn, step - 1)
        return remote(
            total.at[at],
            total.at[at],
            all_send.at[lane, step],
            all_recv.at[lane, step],
            after if turn == 1 else before,
        )

    def add(lane, at, target, extra):
        mine, theirs = views[lane][2].at[at], views[lane][3].at[at]

        def rows(index, carry):
            span = pl.ds(pl.multiple_of(index * 16, 16), 16)
            value = mine[span].astype(jnp.float32) + theirs[span].astype(jnp.float32)
            if extra is not None:
                value = value + extra[span].astype(jnp.float32)
            target[span] = value.astype(jnp.bfloat16)
            return carry

        lax.fori_loop(0, mine.shape[0] // 16, rows, 0)

    every = range(len(views))

    def start(step, carry):
        for lane in every:
            for copy in fetch(lane, step):
                copy.start()
        return carry

    lax.fori_loop(0, chips, start, 0)

    def ready(lane, step):
        local_copy, from_other = fetch(lane, step)
        local_copy.wait()
        from_other.wait_recv()

    for lane in every:
        ready(lane, 0)
        mine = views[lane][2].at[place]
        add(lane, place, mine, None)
        pass_on(lane, 0, mine).start()

    def hops(step, carry):
        for lane in every:
            slots = views[lane][4]
            ready(lane, step)
            pass_on(lane, step - 1, slots.at[step - 1]).wait_recv()
            add(lane, chunk(-views[lane][0], step), slots.at[step - 1], slots.at[step - 1])
            pass_on(lane, step, slots.at[step - 1]).start()
        return carry

    lax.fori_loop(1, chips - 1, hops, 0)
    for lane in every:
        slots = views[lane][4]
        ready(lane, chips - 1)
        pass_on(lane, chips - 2, slots.at[chips - 2]).wait_recv()
        at = chunk(-views[lane][0], chips - 1)
        add(lane, at, views[lane][5].at[at], slots.at[chips - 2])
        share(lane, 0).start()

    def shares(step, carry):
        for lane in every:
            share(lane, step - 1).wait_recv()
            share(lane, step).start()
        return carry

    lax.fori_loop(1, chips - 1, shares, 0)
    for lane in every:
        share(lane, chips - 2).wait_recv()

    def sent(step, carry):
        for lane in every:
            pass_on(lane, step, views[lane][4].at[step]).wait_send()
            share(lane, step).wait_send()
            fetch(lane, step)[1].wait_send()
        return carry

    lax.fori_loop(0, chips - 1, sent, 0)
    for lane in every:
        fetch(lane, chips - 1)[1].wait_send()


def ring_sum(big, tiny):
    _, lanes, chips, rows, width = big.shape
    _, _, low_rows, low_width = tiny.shape
    whole, low_whole = (lanes, chips, rows, width), (chips, low_rows, low_width)
    sems = pltpu.SemaphoreType.DMA((lanes + 1, chips))
    return pl.pallas_call(
        partial(ring_kernel, chips),
        out_shape=(
            jax.ShapeDtypeStruct(whole, jnp.bfloat16),
            jax.ShapeDtypeStruct(low_whole, jnp.bfloat16),
        ),
        in_specs=[pl.BlockSpec(memory_space=pl.ANY)] * 2,
        out_specs=[pl.BlockSpec(memory_space=pltpu.VMEM)] * 2,
        scratch_shapes=[
            pltpu.VMEM(whole, jnp.bfloat16),
            pltpu.VMEM(low_whole, jnp.bfloat16),
            pltpu.VMEM(whole, jnp.bfloat16),
            pltpu.VMEM(low_whole, jnp.bfloat16),
            pltpu.VMEM((lanes, chips - 1, rows, width), jnp.bfloat16),
            pltpu.VMEM((chips - 1, low_rows, low_width), jnp.bfloat16),
        ]
        + [sems] * 7,
        compiler_params=pltpu.CompilerParams(
            collective_id=0, has_side_effects=True, vmem_limit_bytes=58 * 2**20
        ),
        name="ring_sum",
    )(big, tiny)


def by_width(grad, fsdp, width):
    rows, columns = grad.shape
    cut = grad.astype(jnp.bfloat16).reshape(fsdp, rows // fsdp, columns // width, width)
    return cut.transpose(0, 2, 1, 3).reshape(fsdp, -1, width)


def local(
    tokens,
    grad_out,
    ln1_gain,
    ln1_bias,
    w_qkv,
    b_query,
    b_value,
    w_out,
    b_out,
    ln2_gain,
    ln2_bias,
    w_fc,
    b_fc,
    w_proj,
    b_proj,
):
    fsdp = lax.axis_size("fsdp")
    chips = lax.axis_size("ctx")
    vectors = (ln1_gain, ln1_bias, b_query, b_value, b_out, ln2_gain, ln2_bias, b_proj, b_fc)
    edges = [0]
    for item in vectors:
        edges.append(edges[-1] + item.shape[0])
    wide_qkv = lax.all_gather(w_qkv, "fsdp", axis=0, tiled=True)
    joined = lax.all_gather(jnp.concatenate(vectors).reshape(-1, 128), "fsdp", axis=0, tiled=True)
    joined = joined.reshape(fsdp, edges[-1])
    (gain_one, shift_one, bias_query, bias_value, bias_out, gain_two, shift_two, bias_proj, bias_fc) = (
        joined[:, at:to].reshape(-1) for at, to in zip(edges[:-1], edges[1:])
    )
    wide_out = lax.all_gather(w_out, "fsdp", axis=0, tiled=True)
    wide_fc = lax.all_gather(w_fc, "fsdp", axis=0, tiled=True)
    wide_proj = lax.all_gather(w_proj, "fsdp", axis=0, tiled=True)
    gain_one = gain_one.astype(jnp.float32)
    shift_one = shift_one.astype(jnp.float32)
    gain_two = gain_two.astype(jnp.float32)
    shift_two = shift_two.astype(jnp.float32)
    seqs, block, width = tokens.shape
    rows = seqs * block
    heads = HEADS
    head_size = width // heads
    scale = 1.0 / math.sqrt(head_size)
    inputs = tokens.astype(jnp.float32).reshape(rows, width)
    low_one = norm(inputs, gain_one, shift_one).astype(jnp.bfloat16)
    packed = jnp.dot(low_one, wide_qkv, preferred_element_type=jnp.float32)
    query = (packed[:, :width] + bias_query.astype(jnp.float32)).astype(jnp.bfloat16)
    keys = packed[:, width : 2 * width].astype(jnp.bfloat16)
    values = (packed[:, 2 * width :] + bias_value.astype(jnp.float32)).astype(jnp.bfloat16)
    query = query * jnp.asarray(scale, jnp.bfloat16)
    shape = (seqs, block, width)
    packed_heads = to_heads(
        (query.reshape(shape), keys.reshape(shape), values.reshape(shape)), chips
    )
    attended, kept, row_lse = attend_forward(packed_heads, head_size)
    low_att = to_tokens(attended[:, None], seqs, width)[0]
    mixed = (
        inputs
        + jnp.dot(low_att, wide_out, preferred_element_type=jnp.float32)
        + bias_out.astype(jnp.float32)
    )
    low_two = norm(mixed, gain_two, shift_two).astype(jnp.bfloat16)
    hidden = jnp.dot(low_two, wide_fc, preferred_element_type=jnp.float32) + bias_fc.astype(
        jnp.float32
    )
    low_act = jax.nn.gelu(hidden, approximate=True).astype(jnp.bfloat16)
    result = (
        mixed
        + jnp.dot(low_act, wide_proj, preferred_element_type=jnp.float32)
        + bias_proj.astype(jnp.float32)
    )
    output = result.astype(jnp.bfloat16).reshape(seqs, block, width)
    grad_rows = grad_out.reshape(rows, width)
    grad_float = grad_rows.astype(jnp.float32)
    grad_b_proj = jnp.sum(grad_float, axis=0)
    grad_w_proj = inner(low_act, grad_rows)
    grad_act = times_transposed(grad_rows, wide_proj)
    _, gelu_back = jax.vjp(partial(jax.nn.gelu, approximate=True), hidden)
    low_hidden = gelu_back(grad_act)[0].astype(jnp.bfloat16)
    grad_b_fc = jnp.sum(low_hidden.astype(jnp.float32), axis=0)
    grad_w_fc = inner(low_two, low_hidden)
    grad_normed_two = times_transposed(low_hidden, wide_fc)
    _, norm_two_back = jax.vjp(norm, mixed, gain_two, shift_two)
    grad_mixed_part, grad_ln2_gain, grad_ln2_bias = norm_two_back(grad_normed_two)
    grad_mixed = grad_float + grad_mixed_part
    low_branch = grad_mixed.astype(jnp.bfloat16)
    grad_b_out = jnp.sum(low_branch.astype(jnp.float32), axis=0)
    grad_w_out = inner(low_att, low_branch)
    low_grad_att = times_transposed(low_branch, wide_out).astype(jnp.bfloat16).reshape(shape)
    grad_heads = to_heads((low_grad_att,), chips)[:, 0]
    grads = attend_backward(packed_heads, grad_heads, kept, row_lse, head_size)
    low_grad_query, low_grad_keys, low_grad_values = to_tokens(grads, seqs, width)
    grad_b_query = jnp.sum(low_grad_query.astype(jnp.float32), axis=0)
    grad_b_value = jnp.sum(low_grad_values.astype(jnp.float32), axis=0)
    grad_packed = jnp.concatenate([low_grad_query, low_grad_keys, low_grad_values], axis=1)
    grad_w_qkv = inner(low_one, grad_packed)
    grad_normed_one = times_transposed(grad_packed, wide_qkv)
    _, norm_one_back = jax.vjp(norm, inputs, gain_one, shift_one)
    grad_input_part, grad_ln1_gain, grad_ln1_bias = norm_one_back(grad_normed_one)
    grad_tokens = (grad_mixed + grad_input_part).astype(jnp.bfloat16).reshape(seqs, block, width)
    small = (
        grad_ln1_gain,
        grad_ln1_bias,
        grad_b_query,
        grad_b_value,
        grad_b_out,
        grad_ln2_gain,
        grad_ln2_bias,
        grad_b_proj,
        grad_b_fc,
    )
    small = jnp.concatenate([item.reshape(fsdp, -1) for item in small], axis=1)
    small = small.reshape(fsdp, -1, 128)
    grads = (grad_w_fc, grad_w_proj, grad_w_qkv, grad_w_out)
    shards = (w_fc, w_proj, w_qkv, w_out)
    if fsdp == 2 and chips % 4 == 0 and w_out.size % (4 * chips * 16) == 0 and chips <= 16:
        small = small.astype(jnp.bfloat16)
        spare = -small.shape[1] % (16 * chips)
        small = jnp.pad(small, ((0, 0), (0, spare), (0, 0))).reshape(fsdp, chips, -1, 128)
        big = jnp.concatenate([by_width(item, fsdp, width) for item in grads], axis=1)
        big, rest = ring_sum(big.reshape(fsdp, 4, chips, -1, width), small)
        big, totals, at = big.reshape(-1, width), [], 0
        for shard in shards:
            count = shard.size // width
            item = big[at : at + count].reshape(-1, shard.shape[0], width).transpose(1, 0, 2)
            totals.append(item.reshape(shard.shape).astype(jnp.float32))
            at += count
        rest = rest.reshape(-1).astype(jnp.float32)
    else:
        spare = -small.shape[1] % (16 * chips)
        small = jnp.pad(small, ((0, 0), (0, spare), (0, 0)))
        rest = reduce_rows(small.reshape(-1, 128)).reshape(-1).astype(jnp.float32)
        totals = [reduce_rows(item).astype(jnp.float32) for item in grads]
    total_fc, total_proj, total_qkv, total_out = totals
    part = [rest[at:to] for at, to in zip(edges[:-1], edges[1:])]
    return (
        output,
        grad_tokens,
        part[0],
        part[1],
        total_qkv,
        part[2],
        part[3],
        total_out,
        part[4],
        part[5],
        part[6],
        total_fc,
        part[8],
        total_proj,
        part[7],
    )


def solution(mesh):
    in_specs = (
        P("fsdp", "ctx", None),
        P("fsdp", "ctx", None),
        P("fsdp"),
        P("fsdp"),
        P("fsdp", None),
        P("fsdp"),
        P("fsdp"),
        P("fsdp", None),
        P("fsdp"),
        P("fsdp"),
        P("fsdp"),
        P("fsdp", None),
        P("fsdp"),
        P("fsdp", None),
        P("fsdp"),
    )
    out_specs = (
        P("fsdp", "ctx", None),
        P("fsdp", "ctx", None),
        P("fsdp"),
        P("fsdp"),
        P("fsdp", None),
        P("fsdp"),
        P("fsdp"),
        P("fsdp", None),
        P("fsdp"),
        P("fsdp"),
        P("fsdp"),
        P("fsdp", None),
        P("fsdp"),
        P("fsdp", None),
        P("fsdp"),
    )
    return jax.shard_map(local, mesh=mesh, in_specs=in_specs, out_specs=out_specs, check_vma=False)
```

```python
from functools import partial
import math

import jax
import jax.numpy as jnp
from jax import lax
from jax.experimental import pallas as pl
from jax.experimental.pallas import tpu as pltpu
from jax.sharding import PartitionSpec as P

HEADS = 16


def norm(inputs, gain, shift):
    mean = jnp.mean(inputs, axis=-1, keepdims=True)
    centred = inputs - mean
    spread = jnp.mean(centred * centred, axis=-1, keepdims=True)
    return centred * lax.rsqrt(spread + 1e-05) * gain + shift


def inner(left, right):
    return lax.dot_general(
        left, right, (((0,), (0,)), ((), ())), preferred_element_type=jnp.float32
    )


def times_transposed(left, right):
    return lax.dot_general(
        left, right, (((1,), (1,)), ((), ())), preferred_element_type=jnp.float32
    )


def dot_nt(left, right):
    return lax.dot_general(
        left, right, (((1,), (1,)), ((), ())), preferred_element_type=jnp.float32
    )


def dot_nn(left, right):
    return jnp.dot(left, right, preferred_element_type=jnp.float32)


def causal(scores_t, start):
    rows, size = scores_t.shape
    key = lax.broadcasted_iota(jnp.int32, (size, size), 0)
    pos = lax.broadcasted_iota(jnp.int32, (size, size), 1)
    last = jnp.where(key <= pos, scores_t[start:], -1e30)
    if start == 0:
        return last
    return jnp.concatenate([scores_t[:start], last], axis=0)


def forward_kernel(head_size, size, packed_ref, out_ref, keep_ref, lse_ref):
    chips, _, block, span = packed_ref.shape
    length = chips * block
    query = packed_ref[:, 0].reshape(length, span)
    keys = packed_ref[:, 1].reshape(length, span)
    values = packed_ref[:, 2].reshape(length, span)
    for first in range(0, length, size):
        stop = first + size
        parts = []
        for head in range(span // head_size):
            cols = slice(head * head_size, (head + 1) * head_size)
            scores = causal(dot_nt(keys[:stop, cols], query[first:stop, cols]), first)
            top = jnp.max(scores, axis=0, keepdims=True)
            weights = jnp.exp(scores - top)
            total = jnp.sum(weights, axis=0, keepdims=True)
            summed = lax.dot_general(
                values[:stop, cols],
                weights.astype(jnp.bfloat16),
                (((0,), (0,)), ((), ())),
                preferred_element_type=jnp.float32,
            )
            attended = summed / total
            keep_ref[head, :, first:stop] = attended
            lse_ref[head, :, first:stop] = top + jnp.log(total)
            parts.append(attended)
        joined = parts[0] if len(parts) == 1 else jnp.concatenate(parts, axis=0)
        out_ref[first // block : stop // block] = (
            joined.T.astype(jnp.bfloat16).reshape(size // block, block, span)
        )


def backward_kernel(head_size, size, packed_ref, grad_ref, keep_ref, lse_ref, out_ref, key_acc, value_acc):
    chips, _, block, span = packed_ref.shape
    length = chips * block
    query = packed_ref[:, 0].reshape(length, span)
    keys = packed_ref[:, 1].reshape(length, span)
    values = packed_ref[:, 2].reshape(length, span)
    grads = grad_ref[...].reshape(length, span)
    key_acc[...] = jnp.zeros_like(key_acc)
    value_acc[...] = jnp.zeros_like(value_acc)
    for first in range(0, length, size):
        stop = first + size
        grad_t = grads[first:stop].astype(jnp.float32).T
        parts = []
        for head in range(span // head_size):
            cols = slice(head * head_size, (head + 1) * head_size)
            q, do = query[first:stop, cols], grads[first:stop, cols]
            k, v = keys[:stop, cols], values[:stop, cols]
            delta = jnp.sum(grad_t[cols] * keep_ref[head, :, first:stop], axis=0, keepdims=True)
            scores = causal(dot_nt(k, q), first)
            probs = jnp.exp(scores - lse_ref[head, :, first:stop])
            value_acc[head, :stop] += dot_nn(probs.astype(jnp.bfloat16), do)
            slopes = (probs * (dot_nt(v, do) - delta)).astype(jnp.bfloat16)
            key_acc[head, :stop] += dot_nn(slopes, q)
            parts.append(
                lax.dot_general(
                    k, slopes, (((0,), (0,)), ((), ())), preferred_element_type=jnp.float32
                )
            )
        joined = parts[0] if len(parts) == 1 else jnp.concatenate(parts, axis=0)
        grad_query = (joined * (1.0 / math.sqrt(head_size))).T
        out_ref[first // block : stop // block, 0] = (
            grad_query.astype(jnp.bfloat16).reshape(size // block, block, span)
        )
    for at, acc in ((1, key_acc), (2, value_acc)):
        heads = [acc[head] for head in range(span // head_size)]
        whole = heads[0] if len(heads) == 1 else jnp.concatenate(heads, axis=1)
        out_ref[:, at] = whole.astype(jnp.bfloat16).reshape(chips, block, span)


def attend_forward(packed, head_size):
    chips, _, block, span = packed.shape
    length, heads = chips * block, span // head_size
    pairs = heads * length * length
    return pl.pallas_call(
        partial(forward_kernel, head_size, min(512, length)),
        out_shape=(
            jax.ShapeDtypeStruct((chips, block, span), jnp.bfloat16),
            jax.ShapeDtypeStruct((heads, head_size, length), jnp.float32),
            jax.ShapeDtypeStruct((heads, 1, length), jnp.float32),
        ),
        compiler_params=pltpu.CompilerParams(vmem_limit_bytes=56 * 2**20),
        cost_estimate=pl.CostEstimate(
            flops=3 * pairs * head_size, bytes_accessed=6 * packed.size, transcendentals=pairs
        ),
        name="attend_forward",
    )(packed)


def attend_backward(packed, grads, kept, lse, head_size):
    chips, _, block, span = packed.shape
    length, heads = chips * block, span // head_size
    pairs = heads * length * length
    return pl.pallas_call(
        partial(backward_kernel, head_size, min(512, length)),
        out_shape=jax.ShapeDtypeStruct(packed.shape, jnp.bfloat16),
        scratch_shapes=[
            pltpu.VMEM((heads, length, head_size), jnp.float32),
            pltpu.VMEM((heads, length, head_size), jnp.float32),
        ],
        compiler_params=pltpu.CompilerParams(vmem_limit_bytes=56 * 2**20),
        cost_estimate=pl.CostEstimate(
            flops=8 * pairs * head_size, bytes_accessed=8 * packed.size, transcendentals=pairs
        ),
        name="attend_backward",
    )(packed, grads, kept, lse)


def to_heads(arrays, chips):
    seqs, block, width = arrays[0].shape
    span = seqs * width // chips
    parts = [
        item.reshape(seqs, block, width // span, span)
        .transpose(0, 2, 1, 3)
        .reshape(chips, block, span)
        for item in arrays
    ]
    return lax.all_to_all(jnp.stack(parts, axis=1), "ctx", 0, 0, tiled=True)


def to_tokens(item, seqs, width):
    chips, count, block, span = item.shape
    back = lax.all_to_all(item, "ctx", 0, 0, tiled=True)
    back = back.reshape(seqs, width // span, count, block, span).transpose(2, 0, 3, 1, 4)
    return back.reshape(count, seqs * block, width)


def reduce_rows(grad):
    part = lax.psum_scatter(grad.astype(jnp.bfloat16), "fsdp", scatter_dimension=0, tiled=True)
    part = lax.psum_scatter(part, "ctx", scatter_dimension=0, tiled=True)
    return lax.all_gather(part, "ctx", axis=0, tiled=True)


def ring_place(at):
    z, y, x = at // 4, (at // 2) % 2, at % 2
    column = y * (3 - x) + (1 - y) * x
    return column, z


def ring_kernel(
    chips, big, tiny, sum_big, sum_tiny, own, own_tiny, met, met_tiny, hop, hop_tiny,
    own_sem, met_send, met_recv, hop_send, hop_recv, all_send, all_recv,
):
    depth = chips // 4
    core = lax.axis_index("fsdp")
    column, z = ring_place(lax.axis_index("ctx"))
    odd = column % 2
    place = column * depth + (1 - odd) * z + odd * (depth - 1 - z)

    def device(spot):
        column, z = spot // depth, spot % depth
        odd = column % 2
        z = (1 - odd) * z + odd * (depth - 1 - z)
        return {"ctx": z * 4 + (column // 2) * 2 + ((column + 1) // 2) % 2}

    after, before = device((place + 1) % chips), device((place + chips - 1) % chips)
    other = {"fsdp": 1 - core}
    barrier = pltpu.get_barrier_semaphore()
    for peer in (after, before, other):
        pl.semaphore_signal(barrier, inc=1, device_id=peer, device_id_type=pl.DeviceIdType.MESH)
    pl.semaphore_wait(barrier, 3)

    lanes = big.shape[1]
    views = []
    for lane in range(lanes):
        views.append(
            (
                1 - 2 * (lane % 2),
                lambda half, at, lane=lane: big.at[half, lane, at],
                own.at[lane],
                met.at[lane],
                hop.at[lane],
                sum_big.at[lane],
            )
        )
    views.append(
        (1, lambda half, at: tiny.at[half, at], own_tiny, met_tiny, hop_tiny, sum_tiny)
    )

    def chunk(turn, step):
        return (place + turn * step + 2 * chips) % chips

    def remote(source, target, send, recv, peer):
        return pltpu.make_async_remote_copy(
            src_ref=source,
            dst_ref=target,
            send_sem=send,
            recv_sem=recv,
            device_id=peer,
            device_id_type=pl.DeviceIdType.MESH,
        )

    def fetch(lane, step):
        turn, source, mine, theirs, _, _ = views[lane]
        at = chunk(-turn, step)
        return (
            pltpu.make_async_copy(source(core, at), mine.at[at], own_sem.at[lane, step]),
            remote(
                source(1 - core, at),
                theirs.at[at],
                met_send.at[lane, step],
                met_recv.at[lane, step],
                other,
            ),
        )

    def pass_on(lane, step, source):
        turn, slots = views[lane][0], views[lane][4]
        return remote(
            source,
            slots.at[step],
            hop_send.at[lane, step],
            hop_recv.at[lane, step],
            after if turn == 1 else before,
        )

    def share(lane, step):
        turn, total = views[lane][0], views[lane][5]
        at = chunk(-turn, step - 1)
        return remote(
            total.at[at],
            total.at[at],
            all_send.at[lane, step],
            all_recv.at[lane, step],
            after if turn == 1 else before,
        )

    def add(lane, at, target, extra):
        mine, theirs = views[lane][2].at[at], views[lane][3].at[at]

        def rows(index, carry):
            span = pl.ds(pl.multiple_of(index * 16, 16), 16)
            value = mine[span].astype(jnp.float32) + theirs[span].astype(jnp.float32)
            if extra is not None:
                value = value + extra[span].astype(jnp.float32)
            target[span] = value.astype(jnp.bfloat16)
            return carry

        lax.fori_loop(0, mine.shape[0] // 16, rows, 0)

    every = range(len(views))

    def start(step, carry):
        for lane in every:
            for copy in fetch(lane, step):
                copy.start()
        return carry

    lax.fori_loop(0, chips, start, 0)

    def ready(lane, step):
        local_copy, from_other = fetch(lane, step)
        local_copy.wait()
        from_other.wait_recv()

    for lane in every:
        ready(lane, 0)
        mine = views[lane][2].at[place]
        add(lane, place, mine, None)
        pass_on(lane, 0, mine).start()

    def hops(step, carry):
        for lane in every:
            slots = views[lane][4]
            ready(lane, step)
            pass_on(lane, step - 1, slots.at[step - 1]).wait_recv()
            add(lane, chunk(-views[lane][0], step), slots.at[step - 1], slots.at[step - 1])
            pass_on(lane, step, slots.at[step - 1]).start()
        return carry

    lax.fori_loop(1, chips - 1, hops, 0)
    for lane in every:
        slots = views[lane][4]
        ready(lane, chips - 1)
        pass_on(lane, chips - 2, slots.at[chips - 2]).wait_recv()
        at = chunk(-views[lane][0], chips - 1)
        add(lane, at, views[lane][5].at[at], slots.at[chips - 2])
        share(lane, 0).start()

    def shares(step, carry):
        for lane in every:
            share(lane, step - 1).wait_recv()
            share(lane, step).start()
        return carry

    lax.fori_loop(1, chips - 1, shares, 0)
    for lane in every:
        share(lane, chips - 2).wait_recv()

    def sent(step, carry):
        for lane in every:
            pass_on(lane, step, views[lane][4].at[step]).wait_send()
            share(lane, step).wait_send()
            fetch(lane, step)[1].wait_send()
        return carry

    lax.fori_loop(0, chips - 1, sent, 0)
    for lane in every:
        fetch(lane, chips - 1)[1].wait_send()


def ring_sum(big, tiny):
    _, lanes, chips, rows, width = big.shape
    _, _, low_rows, low_width = tiny.shape
    whole, low_whole = (lanes, chips, rows, width), (chips, low_rows, low_width)
    sems = pltpu.SemaphoreType.DMA((lanes + 1, chips))
    return pl.pallas_call(
        partial(ring_kernel, chips),
        out_shape=(
            jax.ShapeDtypeStruct(whole, jnp.bfloat16),
            jax.ShapeDtypeStruct(low_whole, jnp.bfloat16),
        ),
        in_specs=[pl.BlockSpec(memory_space=pl.ANY)] * 2,
        out_specs=[pl.BlockSpec(memory_space=pltpu.VMEM)] * 2,
        scratch_shapes=[
            pltpu.VMEM(whole, jnp.bfloat16),
            pltpu.VMEM(low_whole, jnp.bfloat16),
            pltpu.VMEM(whole, jnp.bfloat16),
            pltpu.VMEM(low_whole, jnp.bfloat16),
            pltpu.VMEM((lanes, chips - 1, rows, width), jnp.bfloat16),
            pltpu.VMEM((chips - 1, low_rows, low_width), jnp.bfloat16),
        ]
        + [sems] * 7,
        compiler_params=pltpu.CompilerParams(
            collective_id=0, has_side_effects=True, vmem_limit_bytes=58 * 2**20
        ),
        name="ring_sum",
    )(big, tiny)


def by_width(grad, fsdp, width):
    rows, columns = grad.shape[0] // fsdp, grad.shape[1]
    low = grad.astype(jnp.bfloat16)
    return [
        [low[half * rows : (half + 1) * rows, at : at + width] for at in range(0, columns, width)]
        for half in range(fsdp)
    ]


def local(
    tokens,
    grad_out,
    ln1_gain,
    ln1_bias,
    w_qkv,
    b_query,
    b_value,
    w_out,
    b_out,
    ln2_gain,
    ln2_bias,
    w_fc,
    b_fc,
    w_proj,
    b_proj,
):
    fsdp = lax.axis_size("fsdp")
    chips = lax.axis_size("ctx")
    vectors = (ln1_gain, ln1_bias, b_query, b_value, b_out, ln2_gain, ln2_bias, b_proj, b_fc)
    edges = [0]
    for item in vectors:
        edges.append(edges[-1] + item.shape[0])
    wide_qkv = lax.all_gather(w_qkv, "fsdp", axis=0, tiled=True)
    joined = lax.all_gather(jnp.concatenate(vectors).reshape(-1, 128), "fsdp", axis=0, tiled=True)
    joined = joined.reshape(fsdp, edges[-1])
    (gain_one, shift_one, bias_query, bias_value, bias_out, gain_two, shift_two, bias_proj, bias_fc) = (
        joined[:, at:to].reshape(-1) for at, to in zip(edges[:-1], edges[1:])
    )
    wide_out = lax.all_gather(w_out, "fsdp", axis=0, tiled=True)
    wide_fc = lax.all_gather(w_fc, "fsdp", axis=0, tiled=True)
    wide_proj = lax.all_gather(w_proj, "fsdp", axis=0, tiled=True)
    gain_one = gain_one.astype(jnp.float32)
    shift_one = shift_one.astype(jnp.float32)
    gain_two = gain_two.astype(jnp.float32)
    shift_two = shift_two.astype(jnp.float32)
    seqs, block, width = tokens.shape
    rows = seqs * block
    heads = HEADS
    head_size = width // heads
    scale = 1.0 / math.sqrt(head_size)
    inputs = tokens.astype(jnp.float32).reshape(rows, width)
    low_one = norm(inputs, gain_one, shift_one).astype(jnp.bfloat16)
    packed = jnp.dot(low_one, wide_qkv, preferred_element_type=jnp.float32)
    query = (packed[:, :width] + bias_query.astype(jnp.float32)).astype(jnp.bfloat16)
    keys = packed[:, width : 2 * width].astype(jnp.bfloat16)
    values = (packed[:, 2 * width :] + bias_value.astype(jnp.float32)).astype(jnp.bfloat16)
    query = query * jnp.asarray(scale, jnp.bfloat16)
    shape = (seqs, block, width)
    packed_heads = to_heads(
        (query.reshape(shape), keys.reshape(shape), values.reshape(shape)), chips
    )
    attended, kept, row_lse = attend_forward(packed_heads, head_size)
    low_att = to_tokens(attended[:, None], seqs, width)[0]
    mixed = (
        inputs
        + jnp.dot(low_att, wide_out, preferred_element_type=jnp.float32)
        + bias_out.astype(jnp.float32)
    )
    low_two = norm(mixed, gain_two, shift_two).astype(jnp.bfloat16)
    hidden = jnp.dot(low_two, wide_fc, preferred_element_type=jnp.float32) + bias_fc.astype(
        jnp.float32
    )
    low_act = jax.nn.gelu(hidden, approximate=True).astype(jnp.bfloat16)
    result = (
        mixed
        + jnp.dot(low_act, wide_proj, preferred_element_type=jnp.float32)
        + bias_proj.astype(jnp.float32)
    )
    output = result.astype(jnp.bfloat16).reshape(seqs, block, width)
    grad_rows = grad_out.reshape(rows, width)
    grad_float = grad_rows.astype(jnp.float32)
    grad_b_proj = jnp.sum(grad_float, axis=0)
    grad_w_proj = inner(low_act, grad_rows)
    grad_act = times_transposed(grad_rows, wide_proj)
    _, gelu_back = jax.vjp(partial(jax.nn.gelu, approximate=True), hidden)
    low_hidden = gelu_back(grad_act)[0].astype(jnp.bfloat16)
    grad_b_fc = jnp.sum(low_hidden.astype(jnp.float32), axis=0)
    grad_w_fc = inner(low_two, low_hidden)
    grad_normed_two = times_transposed(low_hidden, wide_fc)
    _, norm_two_back = jax.vjp(norm, mixed, gain_two, shift_two)
    grad_mixed_part, grad_ln2_gain, grad_ln2_bias = norm_two_back(grad_normed_two)
    grad_mixed = grad_float + grad_mixed_part
    low_branch = grad_mixed.astype(jnp.bfloat16)
    grad_b_out = jnp.sum(low_branch.astype(jnp.float32), axis=0)
    grad_w_out = inner(low_att, low_branch)
    low_grad_att = times_transposed(low_branch, wide_out).astype(jnp.bfloat16).reshape(shape)
    grad_heads = to_heads((low_grad_att,), chips)[:, 0]
    grads = attend_backward(packed_heads, grad_heads, kept, row_lse, head_size)
    low_grad_query, low_grad_keys, low_grad_values = to_tokens(grads, seqs, width)
    grad_b_query = jnp.sum(low_grad_query.astype(jnp.float32), axis=0)
    grad_b_value = jnp.sum(low_grad_values.astype(jnp.float32), axis=0)
    grad_packed = jnp.concatenate([low_grad_query, low_grad_keys, low_grad_values], axis=1)
    grad_w_qkv = inner(low_one, grad_packed)
    grad_normed_one = times_transposed(grad_packed, wide_qkv)
    _, norm_one_back = jax.vjp(norm, inputs, gain_one, shift_one)
    grad_input_part, grad_ln1_gain, grad_ln1_bias = norm_one_back(grad_normed_one)
    grad_tokens = (grad_mixed + grad_input_part).astype(jnp.bfloat16).reshape(seqs, block, width)
    small = (
        grad_ln1_gain,
        grad_ln1_bias,
        grad_b_query,
        grad_b_value,
        grad_b_out,
        grad_ln2_gain,
        grad_ln2_bias,
        grad_b_proj,
        grad_b_fc,
    )
    small = jnp.concatenate([item.reshape(fsdp, -1) for item in small], axis=1)
    small = small.reshape(fsdp, -1, 128)
    grads = (grad_w_fc, grad_w_proj, grad_w_qkv, grad_w_out)
    shards = (w_fc, w_proj, w_qkv, w_out)
    if fsdp == 2 and chips % 4 == 0 and w_out.size % (4 * chips * 16) == 0 and chips <= 16:
        small = small.astype(jnp.bfloat16)
        spare = -small.shape[1] % (16 * chips)
        small = jnp.pad(small, ((0, 0), (0, spare), (0, 0))).reshape(fsdp, chips, -1, 128)
        cuts = [by_width(item, fsdp, width) for item in grads]
        big = jnp.concatenate(
            [piece for half in range(fsdp) for cut in cuts for piece in cut[half]], axis=0
        )
        big, rest = ring_sum(big.reshape(fsdp, 4, chips, -1, width), small)
        big, totals, at = big.reshape(-1, width), [], 0
        for shard in shards:
            count = shard.size // width
            item = [
                big[row : row + shard.shape[0]].astype(jnp.float32)
                for row in range(at, at + count, shard.shape[0])
            ]
            totals.append(item[0] if len(item) == 1 else jnp.concatenate(item, axis=1))
            at += count
        rest = rest.reshape(-1).astype(jnp.float32)
    else:
        spare = -small.shape[1] % (16 * chips)
        small = jnp.pad(small, ((0, 0), (0, spare), (0, 0)))
        rest = reduce_rows(small.reshape(-1, 128)).reshape(-1).astype(jnp.float32)
        totals = [reduce_rows(item).astype(jnp.float32) for item in grads]
    total_fc, total_proj, total_qkv, total_out = totals
    part = [rest[at:to] for at, to in zip(edges[:-1], edges[1:])]
    return (
        output,
        grad_tokens,
        part[0],
        part[1],
        total_qkv,
        part[2],
        part[3],
        total_out,
        part[4],
        part[5],
        part[6],
        total_fc,
        part[8],
        total_proj,
        part[7],
    )


def solution(mesh):
    in_specs = (
        P("fsdp", "ctx", None),
        P("fsdp", "ctx", None),
        P("fsdp"),
        P("fsdp"),
        P("fsdp", None),
        P("fsdp"),
        P("fsdp"),
        P("fsdp", None),
        P("fsdp"),
        P("fsdp"),
        P("fsdp"),
        P("fsdp", None),
        P("fsdp"),
        P("fsdp", None),
        P("fsdp"),
    )
    out_specs = (
        P("fsdp", "ctx", None),
        P("fsdp", "ctx", None),
        P("fsdp"),
        P("fsdp"),
        P("fsdp", None),
        P("fsdp"),
        P("fsdp"),
        P("fsdp", None),
        P("fsdp"),
        P("fsdp"),
        P("fsdp"),
        P("fsdp", None),
        P("fsdp"),
        P("fsdp", None),
        P("fsdp"),
    )
    return jax.shard_map(local, mesh=mesh, in_specs=in_specs, out_specs=out_specs, check_vma=False)
```
